128 devices in a mesh: patch: 16 (over y, x_lo, core), head: 8 (over z, x_hi).
Axes of the slice: x: 4 (x_hi: 2, x_lo: 2; x = x_hi * 2 + x_lo), y: 4, z: 4, core: 2. Of those that a mesh axis runs over, the one named last changes fastest.
Arguments:
- fresh_qkv: bfloat16 [16384, 3, 24, 128], P(('patch', 'head')), may hold values from -8 to 8
- stale_cache: bfloat16 [16384, 2, 24, 128], P('patch', None, 'head'), may hold values from -8 to 8
- out_weight: bfloat16 [3072, 5120], P('head'), may hold values from -0.4375 to 0.4375
- stream: bfloat16 [16384, 5120], P(('patch', 'head')), may hold values from -1.5 to 1.5
- gate_scale: float32 [5120], replicated, may hold values from 0.1 to 1.9
Outputs:
- block_out: bfloat16 [16384, 5120], P(('patch', 'head'))
- next_cache: bfloat16 [16384, 2, 24, 128], P('patch', None, 'head')
The draws below stay inside these ranges and needn't reach their ends.
All inputs are finite; a program needn't handle non-finite values.
Results may differ from the reference program's by a relative error of at most 0.019.
Values may be sent and summed in bfloat16 or wider, within the bound.
A program may use at most 128 MiB of HBM per device.

```python
import math
import jax
import jax.numpy as jnp
from jax import lax

D = 5120
HS = 128
HEADS = 24
TOKENS = 16384
N_PATCH = 16
N_HEAD = 8


def draw_fresh_qkv(key, part):
    key = jax.random.fold_in(key, 11)
    values_drawn = jnp.clip(jax.random.normal(key, (TOKENS, 3, HEADS, HS), jnp.float32), -3.0, 3.0)
    factors = jnp.array([2.5, 1.0, 1.0], jnp.float32)
    values_drawn = values_drawn * factors[None, :, None, None]
    return values_drawn.astype(jnp.bfloat16)


def draw_stale_cache(key, part):
    key = jax.random.fold_in(key, 12)
    values_drawn = jnp.clip(jax.random.normal(key, (TOKENS, 2, HEADS, HS), jnp.float32), -4.0, 4.0)
    return values_drawn.astype(jnp.bfloat16)


def shard_levels(own_key, extent, shards, least, top_value):
    loudness, own = 1.0, jax.random.fold_in(own_key, 6)
    for position, blocks in shards:
        steps = jnp.exp(jax.random.uniform(jax.random.fold_in(own, position), (blocks,), jnp.float32, least / len(shards), top_value / len(shards)))
        loudness = loudness * jnp.repeat(steps, extent[position] // blocks).reshape([-1 if axis == position else 1 for axis in range(len(extent))])
    return loudness


def noise(stream_key, extent, width, bound, pieces=(), kind=jnp.bfloat16):
    loudness = shard_levels(stream_key, extent, pieces, -0.22, 0.18) if pieces else 1.0
    values = jax.random.normal(stream_key, extent, jnp.float32) * width * loudness
    return jnp.minimum(jnp.maximum(values, -bound), bound).astype(kind)


def setup_inputs(seed: int = 0) -> dict:
    arg_keys = jax.random.split(jax.random.key(seed), 6)
    return {
        "fresh_qkv": draw_fresh_qkv(jax.random.fold_in(arg_keys[5], 71), 0),
        "stale_cache": draw_stale_cache(jax.random.fold_in(arg_keys[5], 71), 0),
        "out_weight": noise(arg_keys[2], (HEADS * HS, D), (HEADS * HS // 16) ** -0.5, 0.4375, ((0, 8),)),
        "stream": noise(arg_keys[3], (TOKENS, D), 0.25, 1.5, ((0, 128),)),
        "gate_scale": jnp.clip(1.0 + 0.18 * jax.random.normal(arg_keys[4], (D,), jnp.float32), 0.1, 1.9),
    }


def reference(fresh_qkv, stale_cache, out_weight, stream, gate_scale):
    span_rows = TOKENS // N_PATCH
    group_heads = HEADS // N_HEAD
    scaling = 1.0 / math.sqrt(HS)

    def per_patch(patch_id):
        row_start = (patch_id * span_rows).astype(jnp.int32)
        fresh_rows = lax.dynamic_slice_in_dim(fresh_qkv, row_start, span_rows, 0)
        keys_vals = lax.dynamic_update_slice_in_dim(stale_cache, fresh_rows[:, 1:], row_start, 0)

        def per_head(head_id):
            queries = lax.dynamic_index_in_dim(fresh_rows[:, 0], head_id, 1, keepdims=False)
            key_rows = lax.dynamic_index_in_dim(keys_vals[:, 0], head_id, 1, keepdims=False)
            value_rows = lax.dynamic_index_in_dim(keys_vals[:, 1], head_id, 1, keepdims=False)
            scores = jnp.dot(queries, key_rows.T, preferred_element_type=jnp.float32) * scaling
            highest = lax.optimization_barrier(jnp.max(scores, axis=1, keepdims=True))
            weights = jnp.exp(scores - highest)
            denominator = lax.optimization_barrier(jnp.sum(weights, axis=1, keepdims=True))
            return jnp.dot(weights.astype(jnp.bfloat16), value_rows, preferred_element_type=jnp.float32) / denominator
        heads_out = lax.map(per_head, jnp.arange(HEADS, dtype=jnp.int32))
        attended = jnp.transpose(heads_out, (1, 0, 2)).astype(jnp.bfloat16).reshape(span_rows, HEADS * HS)
        summed = jnp.zeros((span_rows, D), jnp.float32)
        for group_id in range(N_HEAD):
            first_col = group_id * group_heads * HS
            last_col = first_col + group_heads * HS
            partial_sum = jnp.dot(attended[:, first_col:last_col], out_weight[first_col:last_col], preferred_element_type=jnp.float32).astype(jnp.bfloat16)
            partial_sum = lax.optimization_barrier(partial_sum)
            summed = summed + partial_sum.astype(jnp.float32)
        stream_rows = lax.dynamic_slice_in_dim(stream, row_start, span_rows, 0)
        return (stream_rows.astype(jnp.float32) + gate_scale * summed).astype(jnp.bfloat16)
    outputs = lax.map(per_patch, jnp.arange(N_PATCH, dtype=jnp.int32))
    return (outputs.reshape(TOKENS, D), fresh_qkv[:, 1:])
```

```python
import functools
import math

import jax
import jax.numpy as jnp
from jax import lax
from jax.experimental import pallas as pl
from jax.experimental.pallas import tpu as pltpu
from jax.sharding import PartitionSpec as P

MESH = pl.DeviceIdType.MESH
BF16 = jnp.bfloat16
F32 = jnp.float32

SIB, OWN = 0, 7
UP1, DN1, XN, UP2, XUP1, XDN1, XUP2 = 1, 2, 5, 8, 10, 12, 14
TWIN = {UP1: 3, DN1: 4, XN: 6, UP2: 9, XUP1: 11, XDN1: 13, XUP2: 15}
SEND = {name: i for i, name in enumerate(
    ["own_sib", "own_dn", "own_up", "own_x", "f_up1", "f_xn", "f_dn1", "f_xup1"])}
SIB_SEND = {slot: 8 + i for i, slot in enumerate(TWIN)}


def attention_kernel(fresh, stale, att_out, cache_out, kv, qbuf, acc, high,
                     kv_ss, kv_rs, a2a_ss, a2a_rs, loc):
    rows = 128
    p = lax.axis_index("patch")
    g = lax.axis_index("head")
    y, xl, c = p // 4, (p // 2) % 2, p % 2
    z, xh = g // 2, g % 2
    step_dn = 1 + 2 * c

    def patch_dev(yy, xx, cc):
        return {"patch": (yy * 2 + xx) * 2 + cc, "head": g}

    sib = patch_dev(y, xl, 1 - c)
    dn = patch_dev((y + step_dn) % 4, xl, c)
    up = patch_dev((y + 4 - step_dn) % 4, xl, c)
    xn = patch_dev(y, 1 - xl, c)

    def head_dev(k):
        other = (g + k) % 8
        return {"patch": p, "head": other}, other

    barrier = pltpu.get_barrier_semaphore()
    for dev in (sib, dn, up, xn):
        pl.semaphore_signal(barrier, inc=1, device_id=dev, device_id_type=MESH)
    for k in range(1, 8):
        pl.semaphore_signal(barrier, inc=1, device_id=head_dev(k)[0], device_id_type=MESH)
    pl.semaphore_wait(barrier, 11)

    def q_place(src_z, src_xh, dst_xh):
        same = 1 - (src_xh + dst_xh) % 2
        return pl.multiple_of(same * 512 + src_z * rows, rows)

    def q_send(k):
        dev, other = head_dev(k)
        return pltpu.make_async_remote_copy(
            src_ref=fresh.at[other, :, 0], dst_ref=qbuf.at[:, pl.ds(q_place(z, xh, other % 2), rows)],
            send_sem=a2a_ss.at[0, k], recv_sem=a2a_rs.at[0, k], device_id=dev, device_id_type=MESH)

    def kv_send(k):
        dev, other = head_dev(k)
        return pltpu.make_async_remote_copy(
            src_ref=fresh.at[other, :, 1:3],
            dst_ref=kv.at[OWN, :, :, pl.ds(pl.multiple_of(g * rows, rows), rows)],
            send_sem=a2a_ss.at[1, k], recv_sem=a2a_rs.at[1, k], device_id=dev, device_id_type=MESH)

    q_own = pltpu.make_async_copy(
        fresh.at[g, :, 0], qbuf.at[:, pl.ds(q_place(z, xh, xh), rows)], loc.at[0])
    kv_own = pltpu.make_async_copy(
        fresh.at[g, :, 1:3], kv.at[OWN, :, :, pl.ds(pl.multiple_of(g * rows, rows), rows)], loc.at[1])

    def block_send(kind, src, slot, h, dev):
        return pltpu.make_async_remote_copy(
            src_ref=src, dst_ref=kv.at[slot, h], send_sem=kv_ss.at[kind, h],
            recv_sem=kv_rs.at[slot, h], device_id=dev, device_id_type=MESH)

    def own_sends(h):
        return [block_send(SEND["own_sib"], stale.at[h], SIB, h, sib),
                block_send(SEND["own_dn"], stale.at[h], UP1, h, dn),
                block_send(SEND["own_up"], stale.at[h], DN1, h, up),
                block_send(SEND["own_x"], stale.at[h], XN, h, xn)]

    forwards = {UP1: ("f_up1", UP2, dn), XN: ("f_xn", XUP1, dn),
                DN1: ("f_dn1", XDN1, xn), XUP1: ("f_xup1", XUP2, dn)}

    def arrived(slot, h):
        block_send(0, kv.at[slot, h], slot, h, sib).wait_recv()

    def slot_sends(slot, h):
        out = []
        if slot in forwards:
            name, target, dev = forwards[slot]
            out.append(block_send(SEND[name], kv.at[slot, h], target, h, dev))
        out.append(block_send(SIB_SEND[slot], kv.at[slot, h], TWIN[slot], h, sib))
        return out

    def pump(slot, h):
        arrived(slot, h)
        for copy in slot_sends(slot, h):
            copy.start()

    for k in range(1, 8):
        q_send(k).start()
    q_own.start()
    kv_own.start()
    for copy in own_sends(0):
        copy.start()
    for k in range(1, 8):
        kv_send(k).start()
    for h in (1, 2):
        for copy in own_sends(h):
            copy.start()

    acc[...] = jnp.zeros_like(acc)
    high[...] = jnp.full_like(high, -1e30)
    scale = math.log2(math.e) / math.sqrt(128)

    def attend(h, first):
        def half(j, carry):
            at = pl.ds(pl.multiple_of(j * 512, 512), 512)
            q = qbuf[h, at, :]
            m = high[h, at, :]
            total = acc[h, at, :]
            ones = jnp.ones((2048, 128), BF16)
            scores = []
            for u in range(2):
                keys = kv[first + 2 * u:first + 2 * u + 2, h, 0].reshape(2048, 128)
                scores.append(lax.dot_general(q, keys, (((1,), (1,)), ((), ())), preferred_element_type=F32))
            for u in range(2):
                s = scores[u]
                top = s[:, :128]
                for t in range(1, 16):
                    top = jnp.maximum(top, s[:, t * 128:(t + 1) * 128])
                new = jnp.maximum(m, jnp.max(top, axis=1, keepdims=True))
                shrink = jnp.exp2((m - new) * scale)
                weights = jnp.exp2(s * scale - new * scale).astype(BF16)
                values = kv[first + 2 * u:first + 2 * u + 2, h, 1].reshape(2048, 128)
                total = total * shrink + jnp.dot(
                    weights, jnp.concatenate([values, ones], axis=1), preferred_element_type=F32)
                m = new
            high[h, at, :] = m
            acc[h, at, :] = total
            return carry
        lax.fori_loop(0, 2, half, 0)

    q_own.wait()
    for k in range(1, 8):
        q_send(k).wait_recv()

    for h in range(3):
        for slot in (UP1, DN1, XN):
            pump(slot, h)
        if h > 0:
            pump(XUP1, h - 1)
        for slot in (SIB, 3, 4):
            arrived(slot, h)
        attend(h, 0)
        arrived(6, h)
        if h == 0:
            kv_own.wait()
            for k in range(1, 8):
                kv_send(k).wait_recv()
            next_cache = pltpu.make_async_copy(kv.at[OWN], cache_out, loc.at[2])
            next_cache.start()
        attend(h, 4)
    pump(XUP1, 2)
    for h in range(3):
        for slot in (UP2, XDN1, XUP2):
            pump(slot, h)
        for slot in (9, 11):
            arrived(slot, h)
        attend(h, 8)
        for slot in (13, 15):
            arrived(slot, h)
        attend(h, 12)
    att_out[...] = (acc[:, :, :128] / acc[:, :, 128:]).astype(BF16)

    next_cache.wait()
    for k in range(1, 8):
        q_send(k).wait_send()
        kv_send(k).wait_send()
    for h in range(3):
        for copy in own_sends(h):
            copy.wait_send()
        for slot in TWIN:
            for copy in slot_sends(slot, h):
                copy.wait_send()


def attention(fresh, stale):
    any_ = pl.BlockSpec(memory_space=pl.ANY)
    return pl.pallas_call(
        attention_kernel,
        out_shape=[jax.ShapeDtypeStruct((3, 1024, 128), BF16),
                   jax.ShapeDtypeStruct((3, 2, 1024, 128), BF16)],
        in_specs=[any_, any_],
        out_specs=[pl.BlockSpec(memory_space=pltpu.VMEM), any_],
        scratch_shapes=[
            pltpu.VMEM((16, 3, 2, 1024, 128), BF16),
            pltpu.VMEM((3, 1024, 128), BF16),
            pltpu.VMEM((3, 1024, 256), F32),
            pltpu.VMEM((3, 1024, 1), F32),
            pltpu.SemaphoreType.DMA((15, 3)),
            pltpu.SemaphoreType.DMA((16, 3)),
            pltpu.SemaphoreType.DMA((2, 8)),
            pltpu.SemaphoreType.DMA((2, 8)),
            pltpu.SemaphoreType.DMA((3,)),
        ],
        compiler_params=pltpu.CompilerParams(
            collective_id=0, has_side_effects=True, vmem_limit_bytes=60 * 2**20),
        name="gather_attend",
    )(fresh, stale)


def per_device(fresh_qkv, stale_cache, out_weight, stream, gate_scale):
    fresh = jnp.transpose(fresh_qkv.reshape(128, 3, 8, 3, 128), (2, 3, 1, 0, 4))
    stale = jnp.transpose(stale_cache, (2, 1, 0, 3))
    att, cache = attention(fresh, stale)
    xh = lax.axis_index("head") % 2
    att = att.reshape(3, 2, 4, 128, 128)
    att = jnp.where(xh == 1, att, att[:, ::-1])
    attended = jnp.transpose(att, (2, 1, 3, 0, 4)).reshape(1024, 384)
    summed = lax.psum_scatter(
        jnp.dot(attended, out_weight, preferred_element_type=F32).astype(BF16),
        "head", scatter_dimension=0, tiled=True).astype(F32)
    block_out = (stream.astype(F32) + gate_scale * summed).astype(BF16)
    return (block_out, jnp.transpose(cache, (2, 1, 0, 3)))


def solution(mesh):
    return jax.shard_map(
        per_device,
        mesh=mesh,
        in_specs=(
            P(("patch", "head"), None, None, None),
            P("patch", None, "head", None),
            P("head", None),
            P(("patch", "head"), None),
            P(),
        ),
        out_specs=(P(("patch", "head"), None), P("patch", None, "head", None)),
        check_vma=False,
    )
```

```python
import functools
import math

import jax
import jax.numpy as jnp
from jax import lax
from jax.experimental import pallas as pl
from jax.experimental.pallas import tpu as pltpu
from jax.sharding import PartitionSpec as P

MESH = pl.DeviceIdType.MESH
BF16 = jnp.bfloat16
F32 = jnp.float32

SIB, OWN, XN = 0, 2, 3
UP1, DN1, UP2, XDN1, XUP1, XUP2 = 4, 5, 8, 10, 12, 14
TWIN = {XN: 1, UP1: 6, DN1: 7, UP2: 9, XDN1: 11, XUP1: 13, XUP2: 15}
NEAR, FIRST, THIRD, LAST = 0, 4, 8, 12
KINDS = ["own_sib", "own_dn", "own_up", "own_x", "up1_dn", "xn_dn", "xn_up", "xup1_dn"]
SEND = {name: i for i, name in enumerate(KINDS)}
SIB_SEND = {slot: len(KINDS) + i for i, slot in enumerate(TWIN)}
N_SENDS = len(KINDS) + len(TWIN)
TILES, TILE = 8, 640
CHUNKS, CHUNK = 4, 1280


def block_kernel(fresh, stale, weight, stream, gate, out, cache_out,
                 kv, ext, qbuf, acc, stat, wbuf, abuf, res, psend, prec,
                 kv_ss, kv_rs, in_ss, in_rs, w_ss, w_rs, a_ss, a_rs, p_ss, p_rs, loc):
    rows = 128
    p = lax.axis_index("patch")
    g = lax.axis_index("head")
    y, xl, c = p // 4, (p // 2) % 2, p % 2
    z, xh = g // 2, g % 2
    fwd = 1 + 2 * c
    xp = (y * 2 + 1 - xl) * 2 + c

    def patch_dev(yy, xx, cc):
        return {"patch": (yy * 2 + xx) * 2 + cc, "head": g}

    sib = patch_dev(y, xl, 1 - c)
    dn = patch_dev((y + fwd) % 4, xl, c)
    up = patch_dev((y + 4 - fwd) % 4, xl, c)
    xn = patch_dev(y, 1 - xl, c)

    def head_dev(patch, k):
        return {"patch": patch, "head": (g + k) % 8}

    def z_dev(patch, k):
        return {"patch": patch, "head": ((z + k) % 4) * 2 + xh}

    def signal(dev):
        pl.semaphore_signal(barrier, inc=1, device_id=dev, device_id_type=MESH)

    barrier = pltpu.get_barrier_semaphore()
    for dev in (sib, dn, up, xn):
        signal(dev)
    for k in range(1, 8):
        signal(head_dev(p, k))
        signal(head_dev(xp, k))
    pl.semaphore_wait(barrier, 18)

    def remote(src, dst, ss, rs, dev):
        return pltpu.make_async_remote_copy(
            src_ref=src, dst_ref=dst, send_sem=ss, recv_sem=rs, device_id=dev, device_id_type=MESH)

    far_head = 2 - 2 * xl
    tokens = pl.ds(pl.multiple_of(g * rows, rows), rows)

    def q_place(dst_xh):
        same = 1 - (xh + dst_xh) % 2
        return pl.ds(pl.multiple_of(same * 512 + z * rows, rows), rows)

    def fresh_send(kind, k):
        to = (g + k) % 8
        near = pl.ds(xl, 2)
        if kind == 0:
            src, dst, patch = fresh.at[to, near, 0], qbuf.at[0:2, q_place(to % 2)], p
        elif kind == 1:
            src, dst, patch = fresh.at[to, near, 1:3], kv.at[OWN, :, :, tokens], p
        elif kind == 2:
            src, dst, patch = fresh.at[to, far_head, 1:3], cache_out.at[far_head, :, tokens], p
        elif kind == 3:
            src, dst, patch = fresh.at[to, far_head, 0], qbuf.at[2, q_place(to % 2)], xp
        else:
            src, dst, patch = fresh.at[to, far_head, 1:3], ext.at[1, :, tokens], xp
        if patch is p and k == 0:
            return pltpu.make_async_copy(src, dst, loc.at[kind])
        return remote(src, dst, in_ss.at[kind, k], in_rs.at[kind, k], head_dev(patch, k))

    def fresh_start(kind):
        for k in range(8):
            fresh_send(kind, k).start()

    def fresh_arrived(kind):
        for k in range(8):
            if k == 0 and kind < 3:
                fresh_send(kind, k).wait()
            else:
                fresh_send(kind, k).wait_recv()

    def place(o, side):
        return side if o == 0 else 1 - side

    def block_send(kind, src, slot, o, side, dev):
        return remote(src, kv.at[slot, place(o, side)], kv_ss.at[kind, o], kv_rs.at[slot, o], dev)

    def own_sends(o):
        near = stale.at[2 * xl if o == 0 else 1]
        far = stale.at[far_head if o == 0 else 1]
        return [block_send(SEND["own_dn"], near, UP1, o, xl, dn),
                block_send(SEND["own_up"], near, DN1, o, xl, up),
                block_send(SEND["own_sib"], near, SIB, o, xl, sib),
                block_send(SEND["own_x"], far, XN, o, 1 - xl, xn)]

    routes = {UP1: [("up1_dn", UP2, dn)], XN: [("xn_dn", XUP1, dn), ("xn_up", XDN1, up)],
              XUP1: [("xup1_dn", XUP2, dn)]}

    def arrived(slot, o):
        here = kv.at[slot, place(o, xl)]
        remote(here, here, kv_ss.at[0, o], kv_rs.at[slot, o], sib).wait_recv()

    def slot_sends(slot, o):
        here = kv.at[slot, place(o, xl)]
        out_ = [block_send(SEND[name], here, target, o, xl, dev) for name, target, dev in routes.get(slot, [])]
        return out_ + [block_send(SIB_SEND[slot], here, TWIN[slot], o, xl, sib)]

    def pump(slot, o):
        arrived(slot, o)
        for copy in slot_sends(slot, o):
            copy.start()

    def w_at(origin, core, n):
        return (pl.ds(pl.multiple_of(((z + origin) % 4) * 384 + core * 192, 64), 192),
                pl.ds(n * CHUNK, CHUNK))

    def w_own(n):
        src = weight.at[pl.ds(pl.multiple_of(c * 192, 64), 192), pl.ds(n * CHUNK, CHUNK)]
        dst = wbuf.at[w_at(0, c, n)]
        return [remote(src, dst, w_ss.at[0, n], w_rs.at[0, n], z_dev(p, fwd)),
                remote(src, dst, w_ss.at[1, n], w_rs.at[1, n], z_dev(p, 4 - fwd))]

    def w_origin(i):
        return (4 - fwd, fwd, 2)[i]

    def w_sends(i, n):
        here = wbuf.at[w_at(w_origin(i), c, n)]
        copies = [remote(here, here, w_ss.at[2 + i, n], w_rs.at[3 + i, n], sib)]
        if i == 0:
            copies.insert(0, remote(here, here, w_ss.at[5, n], w_rs.at[2, n], z_dev(p, fwd)))
        return copies

    def w_pump(i, n):
        here = wbuf.at[w_at(w_origin(i), c, n)]
        remote(here, here, w_ss.at[0, n], w_rs.at[i, n], sib).wait_recv()
        for copy in w_sends(i, n):
            copy.start()

    def w_twins(n):
        for i in range(3):
            origin = (fwd, 4 - fwd, 2)[i]
            here = wbuf.at[w_at(origin, 1 - c, n)]
            remote(here, here, w_ss.at[0, n], w_rs.at[3 + i, n], sib).wait_recv()

    own_weight = pltpu.make_async_copy(
        weight, wbuf.at[pl.ds(pl.multiple_of(z * 384, 384), 384)], loc.at[5])
    own_stale = pltpu.make_async_copy(stale.at[2 * xl], ext.at[0], loc.at[6])
    residual = pltpu.make_async_copy(stream, res, loc.at[7])
    next_cache = pltpu.make_async_copy(kv.at[OWN], cache_out.at[pl.ds(xl, 2)], loc.at[8])

    def att_sends(j):
        copies = []
        for k in range(4):
            at = pl.ds(pl.multiple_of(j * 512 + ((z + k) % 4) * rows, rows), rows)
            src, dst = qbuf.at[0:2, at], abuf.at[j, z, pl.ds(xl, 2)]
            if k == 0:
                copies.append(pltpu.make_async_copy(src, dst, loc.at[9 + j]))
            else:
                copies.append(remote(src, dst, a_ss.at[j, 0, k], a_rs.at[j, 0, k], z_dev(p, k)))
            copies.append(remote(qbuf.at[2, at], abuf.at[j, z, 2 * xl],
                                 a_ss.at[j, 1, k], a_rs.at[j, 1, k], z_dev(xp, k)))
        return copies

    def att_arrived(j):
        for i, copy in enumerate(att_sends(j)):
            if i == 0:
                copy.wait()
            else:
                copy.wait_recv()

    scale = math.log2(math.e) / math.sqrt(128)

    def attend(unit, pieces, halves=(0, 2)):
        def half(j, carry):
            at = pl.ds(pl.multiple_of(j * 512, 512), 512)
            q = qbuf[unit, at, :]
            m = stat[unit, at, 0:1]
            total = jnp.concatenate(
                [acc[unit, at, :], jnp.broadcast_to(stat[unit, at, 1:2], (512, 128))], axis=1)
            ones = jnp.ones((2048, 128), BF16)
            scores = []
            for load in pieces:
                scores.append(lax.dot_general(q, load(0), (((1,), (1,)), ((), ())), preferred_element_type=F32))
            for s, load in zip(scores, pieces):
                top = s[:, :128]
                for t in range(1, 16):
                    top = jnp.maximum(top, s[:, t * 128:(t + 1) * 128])
                new = jnp.maximum(m, jnp.max(top, axis=1, keepdims=True))
                shrink = jnp.exp2((m - new) * scale)
                weights = jnp.exp2(s * scale - new * scale).astype(BF16)
                total = total * shrink + jnp.dot(
                    weights, jnp.concatenate([load(1), ones], axis=1), preferred_element_type=F32)
                m = new
            stat[unit, at, 0:1] = m
            stat[unit, at, 1:2] = total[:, 128:129]
            acc[unit, at, :] = total[:, :128]
            return carry
        lax.fori_loop(halves[0], halves[1], half, 0)

    def pair(first, side):
        return lambda i: kv[first:first + 2, side, i].reshape(2048, 128)

    def extra(i):
        return ext[:, i].reshape(2048, 128)

    def chunk(first, o):
        side = place(o, xl)
        return [pair(first, side), pair(first + 2, side)]

    own_a, own_1, far_a = xl, 1 - xl, 2

    def finish(j):
        at = slice(512 * j, 512 * j + 512)
        qbuf[:, at] = (acc[:, at] / stat[:, at, 1:2]).astype(BF16)
        for copy in att_sends(j):
            copy.start()

    def product(j, n):
        left = jnp.concatenate([abuf[j, zz, h] for zz in range(4) for h in range(3)], axis=1)
        return jnp.dot(left, wbuf[:, pl.ds(pl.multiple_of(n * TILE, TILE), TILE)], preferred_element_type=F32)

    def part_send(n):
        return remote(psend.at[n], prec.at[n], p_ss.at[n], p_rs.at[n],
                      {"patch": p, "head": z * 2 + 1 - xh})

    fresh_start(0)
    fresh_start(3)
    for copy in own_sends(0):
        copy.start()
    fresh_start(1)
    fresh_start(4)
    for copy in own_sends(1):
        copy.start()
    own_stale.start()
    fresh_start(2)
    own_weight.start()
    residual.start()
    acc[...] = jnp.zeros_like(acc)
    stat[:, :, 0:1] = jnp.full((3, 1024, 1), -1e30, F32)
    stat[:, :, 1:2] = jnp.zeros((3, 1024, 1), F32)

    def pumps(*which):
        for slot, o in which:
            pump(slot, o)

    fresh_arrived(0)
    fresh_arrived(3)
    pumps((UP1, 0), (DN1, 0))
    arrived(TWIN[UP1], 0)
    arrived(TWIN[DN1], 0)
    attend(own_a, chunk(FIRST, 0))
    pumps((XN, 0))
    attend(far_a, chunk(FIRST, 0))
    pumps((UP1, 1), (DN1, 1), (XN, 1))
    for n in range(CHUNKS):
        for copy in w_own(n):
            copy.start()
    arrived(TWIN[UP1], 1)
    arrived(TWIN[DN1], 1)
    attend(own_1, chunk(FIRST, 1))

    arrived(SIB, 0)
    arrived(TWIN[XN], 0)
    fresh_arrived(1)
    next_cache.start()
    attend(own_a, chunk(NEAR, 0))
    pumps((UP2, 0), (XUP1, 0))
    fresh_arrived(4)
    own_stale.wait()
    attend(far_a, [pair(SIB, xl), extra])
    pumps((UP2, 1), (XDN1, 0))
    arrived(SIB, 1)
    arrived(TWIN[XN], 1)
    attend(own_1, chunk(NEAR, 1))

    pumps((XUP1, 1), (XDN1, 1))
    arrived(TWIN[UP2], 0)
    arrived(TWIN[XDN1], 0)
    attend(own_a, chunk(THIRD, 0))
    w_pump(0, 0)
    w_pump(1, 0)
    w_pump(0, 1)
    w_pump(1, 1)
    attend(far_a, chunk(THIRD, 0))
    pumps((XUP2, 0))
    w_pump(0, 2)
    w_pump(1, 2)
    arrived(TWIN[UP2], 1)
    arrived(TWIN[XDN1], 1)
    attend(own_1, chunk(THIRD, 1))
    pumps((XUP2, 1))
    for o in range(2):
        arrived(TWIN[XUP1], o)
        arrived(TWIN[XUP2], o)
    for j in range(2):
        attend(own_a, chunk(LAST, 0), (j, j + 1))
        if j == 0:
            w_pump(0, 3)
            w_pump(1, 3)
        attend(far_a, chunk(LAST, 0), (j, j + 1))
        attend(own_1, chunk(LAST, 1), (j, j + 1))
        finish(j)

    for n in range(CHUNKS):
        w_pump(2, n)
    own_weight.wait()
    residual.wait()
    att_arrived(0)
    for n in range(CHUNKS):
        w_twins(n)

    def give(n, carry):
        psend[n] = product(0, n).astype(BF16)
        part_send(n).start()
        return carry
    lax.fori_loop(0, TILES, give, 0)
    att_arrived(1)

    def take(n, carry):
        mine = product(1, n)
        part_send(n).wait_recv()
        cols = pl.ds(pl.multiple_of(n * TILE, TILE), TILE)
        summed = mine + prec[n].astype(F32)
        res[:, cols] = (res[:, cols].astype(F32) + gate[:, cols] * summed).astype(BF16)
        return carry
    lax.fori_loop(0, TILES, take, 0)

    result = pltpu.make_async_copy(res, out, loc.at[11])
    result.start()

    result.wait()
    next_cache.wait()
    fresh_arrived(2)
    for kind in range(5):
        for k in range(8):
            if k > 0 or kind > 2:
                fresh_send(kind, k).wait_send()
    for o in range(2):
        for copy in own_sends(o):
            copy.wait_send()
        for slot in TWIN:
            for copy in slot_sends(slot, o):
                copy.wait_send()
    for n in range(CHUNKS):
        for copy in w_own(n):
            copy.wait_send()
        for i in range(3):
            for copy in w_sends(i, n):
                copy.wait_send()
    for j in range(2):
        for copy in att_sends(j)[1:]:
            copy.wait_send()

    def sent(n, carry):
        part_send(n).wait_send()
        return carry
    lax.fori_loop(0, TILES, sent, 0)


def block(fresh, stale, weight, stream, gate):
    any_ = pl.BlockSpec(memory_space=pl.ANY)
    vmem = pl.BlockSpec(memory_space=pltpu.VMEM)
    dma = pltpu.SemaphoreType.DMA
    return pl.pallas_call(
        block_kernel,
        out_shape=[jax.ShapeDtypeStruct((128, 5120), BF16),
                   jax.ShapeDtypeStruct((3, 2, 1024, 128), BF16)],
        in_specs=[any_, any_, any_, any_, vmem],
        out_specs=[any_, any_],
        scratch_shapes=[
            pltpu.VMEM((16, 2, 2, 1024, 128), BF16),
            pltpu.VMEM((2, 2, 1024, 128), BF16),
            pltpu.VMEM((3, 1024, 128), BF16),
            pltpu.VMEM((3, 1024, 128), F32),
            pltpu.VMEM((3, 1024, 2), F32),
            pltpu.VMEM((1536, 5120), BF16),
            pltpu.VMEM((2, 4, 3, 128, 128), BF16),
            pltpu.VMEM((128, 5120), BF16),
            pltpu.VMEM((TILES, 128, TILE), BF16),
            pltpu.VMEM((TILES, 128, TILE), BF16),
            dma((N_SENDS, 2)), dma((16, 2)),
            dma((5, 8)), dma((5, 8)),
            dma((6, CHUNKS)), dma((6, CHUNKS)),
            dma((2, 2, 4)), dma((2, 2, 4)),
            dma((TILES,)), dma((TILES,)),
            dma((12,)),
        ],
        compiler_params=pltpu.CompilerParams(
            collective_id=0, has_side_effects=True, vmem_limit_bytes=62 * 2**20),
        name="gather_attend",
    )(fresh, stale, weight, stream, gate)


def per_device(fresh_qkv, stale_cache, out_weight, stream, gate_scale):
    fresh = jnp.transpose(fresh_qkv.reshape(128, 3, 8, 3, 128), (2, 3, 1, 0, 4))
    stale = jnp.transpose(stale_cache, (2, 1, 0, 3))
    block_out, cache = block(fresh, stale, out_weight, stream, gate_scale.reshape(1, -1))
    return (block_out, jnp.transpose(cache, (2, 1, 0, 3)))


def solution(mesh):
    return jax.shard_map(
        per_device,
        mesh=mesh,
        in_specs=(
            P(("patch", "head"), None, None, None),
            P("patch", None, "head", None),
            P("head", None),
            P(("patch", "head"), None),
            P(),
        ),
        out_specs=(P(("patch", "head"), None), P("patch", None, "head", None)),
        check_vma=False,
    )
```

```python
import functools
import math

import jax
import jax.numpy as jnp
from jax import lax
from jax.experimental import pallas as pl
from jax.experimental.pallas import tpu as pltpu
from jax.sharding import PartitionSpec as P

MESH = pl.DeviceIdType.MESH
BF16 = jnp.bfloat16
F32 = jnp.float32

SIB, UP2, UP1, DN1, XDN1, XUP1, OWN, XN, XUP2 = 0, 2, 4, 5, 8, 10, 12, 13, 14
TWIN = {XN: 1, UP2: 3, UP1: 6, DN1: 7, XDN1: 9, XUP1: 11, XUP2: 15}
FIRST, SECOND, THIRD, LAST = 4, 0, 8, 12
KINDS = ["own_sib", "own_dn", "own_up", "own_x", "up1_dn", "xn_dn", "xn_up", "xup1_dn"]
SEND = {name: i for i, name in enumerate(KINDS)}
SIB_SEND = {slot: len(KINDS) + i for i, slot in enumerate(TWIN)}
N_SENDS = len(KINDS) + len(TWIN)
TILES, TILE = 8, 640
CHUNKS, CHUNK = 4, 1280


def block_kernel(fresh, stale, weight, stream, gate, out, cache_out,
                 kv, ext, qbuf, acc, stat, wbuf, abuf, res, psend, prec,
                 kv_ss, kv_rs, in_ss, in_rs, w_ss, w_rs, a_ss, a_rs, p_ss, p_rs, loc):
    rows = 128
    p = lax.axis_index("patch")
    g = lax.axis_index("head")
    y, xl, c = p // 4, (p // 2) % 2, p % 2
    z, xh = g // 2, g % 2
    fwd = 1 + 2 * c
    xp = (y * 2 + 1 - xl) * 2 + c

    def patch_dev(yy, xx, cc):
        return {"patch": (yy * 2 + xx) * 2 + cc, "head": g}

    sib = patch_dev(y, xl, 1 - c)
    dn = patch_dev((y + fwd) % 4, xl, c)
    up = patch_dev((y + 4 - fwd) % 4, xl, c)
    xn = patch_dev(y, 1 - xl, c)

    def head_dev(patch, k):
        return {"patch": patch, "head": (g + k) % 8}

    def z_dev(patch, k):
        return {"patch": patch, "head": ((z + k) % 4) * 2 + xh}

    def signal(dev):
        pl.semaphore_signal(barrier, inc=1, device_id=dev, device_id_type=MESH)

    barrier = pltpu.get_barrier_semaphore()
    for dev in (sib, dn, up, xn):
        signal(dev)
    for k in range(1, 8):
        signal(head_dev(p, k))
        signal(head_dev(xp, k))
    pl.semaphore_wait(barrier, 18)

    def remote(src, dst, ss, rs, dev):
        return pltpu.make_async_remote_copy(
            src_ref=src, dst_ref=dst, send_sem=ss, recv_sem=rs, device_id=dev, device_id_type=MESH)

    far_head = 2 - 2 * xl
    tokens = pl.ds(pl.multiple_of(g * rows, rows), rows)

    def q_place(dst_xh):
        same = 1 - (xh + dst_xh) % 2
        return pl.ds(pl.multiple_of(same * 512 + z * rows, rows), rows)

    def fresh_send(kind, k):
        to = (g + k) % 8
        near = pl.ds(xl, 2)
        if kind == 0:
            src, dst, patch = fresh.at[to, near, 0], qbuf.at[0:2, q_place(to % 2)], p
        elif kind == 1:
            src, dst, patch = fresh.at[to, near, 1:3], kv.at[OWN, :, :, tokens], p
        elif kind == 2:
            src, dst, patch = fresh.at[to, far_head, 0], qbuf.at[2, q_place(to % 2)], xp
        else:
            src, dst, patch = fresh.at[to, far_head, 1:3], ext.at[1, :, tokens], xp
        if patch is p and k == 0:
            return pltpu.make_async_copy(src, dst, loc.at[kind])
        return remote(src, dst, in_ss.at[kind, k], in_rs.at[kind, k], head_dev(patch, k))

    def fresh_start(kind):
        for k in range(8):
            fresh_send(kind, k).start()

    def fresh_arrived(kind):
        for k in range(8):
            if k == 0 and kind < 2:
                fresh_send(kind, k).wait()
            else:
                fresh_send(kind, k).wait_recv()

    def place(o, side):
        return side if o == 0 else 1 - side

    def block_send(kind, src, slot, o, side, dev):
        return remote(src, kv.at[slot, place(o, side)], kv_ss.at[kind, o], kv_rs.at[slot, o], dev)

    def own_sends(o):
        near = stale.at[2 * xl if o == 0 else 1]
        far = stale.at[far_head if o == 0 else 1]
        return [block_send(SEND["own_dn"], near, UP1, o, xl, dn),
                block_send(SEND["own_up"], near, DN1, o, xl, up),
                block_send(SEND["own_sib"], near, SIB, o, xl, sib),
                block_send(SEND["own_x"], far, XN, o, 1 - xl, xn)]

    routes = {UP1: [("up1_dn", UP2, dn)], XN: [("xn_dn", XUP1, dn), ("xn_up", XDN1, up)],
              XUP1: [("xup1_dn", XUP2, dn)]}

    def arrived(slot, o):
        here = kv.at[slot, place(o, xl)]
        remote(here, here, kv_ss.at[0, o], kv_rs.at[slot, o], sib).wait_recv()

    def slot_sends(slot, o):
        here = kv.at[slot, place(o, xl)]
        out_ = [block_send(SEND[name], here, target, o, xl, dev) for name, target, dev in routes.get(slot, [])]
        return out_ + [block_send(SIB_SEND[slot], here, TWIN[slot], o, xl, sib)]

    def pump(slot, o):
        arrived(slot, o)
        for copy in slot_sends(slot, o):
            copy.start()

    def w_at(origin, core, n):
        return (pl.ds(pl.multiple_of(((z + origin) % 4) * 384 + core * 192, 64), 192),
                pl.ds(n * CHUNK, CHUNK))

    def w_own(n):
        src = weight.at[pl.ds(pl.multiple_of(c * 192, 64), 192), pl.ds(n * CHUNK, CHUNK)]
        dst = wbuf.at[w_at(0, c, n)]
        return [remote(src, dst, w_ss.at[0, n], w_rs.at[0, n], z_dev(p, fwd)),
                remote(src, dst, w_ss.at[1, n], w_rs.at[1, n], z_dev(p, 4 - fwd))]

    def w_origin(i):
        return (4 - fwd, fwd, 2)[i]

    def w_sends(i, n):
        here = wbuf.at[w_at(w_origin(i), c, n)]
        copies = [remote(here, here, w_ss.at[2 + i, n], w_rs.at[3 + i, n], sib)]
        if i == 0:
            copies.insert(0, remote(here, here, w_ss.at[5, n], w_rs.at[2, n], z_dev(p, fwd)))
        return copies

    def w_pump(i, n):
        here = wbuf.at[w_at(w_origin(i), c, n)]
        remote(here, here, w_ss.at[0, n], w_rs.at[i, n], sib).wait_recv()
        for copy in w_sends(i, n):
            copy.start()

    def w_twins(n):
        for i in range(3):
            origin = (fwd, 4 - fwd, 2)[i]
            here = wbuf.at[w_at(origin, 1 - c, n)]
            remote(here, here, w_ss.at[0, n], w_rs.at[3 + i, n], sib).wait_recv()

    own_weight = pltpu.make_async_copy(
        weight, wbuf.at[pl.ds(pl.multiple_of(z * 384, 384), 384)], loc.at[5])
    own_stale = pltpu.make_async_copy(stale.at[2 * xl], ext.at[0], loc.at[6])
    residual = pltpu.make_async_copy(stream, res, loc.at[7])
    next_cache = pltpu.make_async_copy(kv.at[OWN], cache_out.at[pl.ds(xl, 2)], loc.at[8])

    far_cache = remote(ext.at[1], cache_out.at[2 * xl], loc.at[2], loc.at[3], xn)

    def att_sends(j):
        copies = []
        for k in range(4):
            at = pl.ds(pl.multiple_of(j * 512 + ((z + k) % 4) * rows, rows), rows)
            src, dst = qbuf.at[0:2, at], abuf.at[j, z, pl.ds(xl, 2)]
            if k == 0:
                copies.append(pltpu.make_async_copy(src, dst, loc.at[9 + j]))
            else:
                copies.append(remote(src, dst, a_ss.at[j, 0, k], a_rs.at[j, 0, k], z_dev(p, k)))
            copies.append(remote(qbuf.at[2, at], abuf.at[j, z, 2 * xl],
                                 a_ss.at[j, 1, k], a_rs.at[j, 1, k], z_dev(xp, k)))
        return copies

    def att_arrived(j):
        for i, copy in enumerate(att_sends(j)):
            if i == 0:
                copy.wait()
            else:
                copy.wait_recv()

    scale = math.log2(math.e) / math.sqrt(128)

    def attend(unit, pieces, halves=(0, 2)):
        def half(j, carry):
            at = pl.ds(pl.multiple_of(j * 512, 512), 512)
            q = qbuf[unit, at, :]
            m = stat[unit, at, 0:1]
            total = jnp.concatenate(
                [acc[unit, at, :], jnp.broadcast_to(stat[unit, at, 1:2], (512, 128))], axis=1)
            ones = jnp.ones((2048, 128), BF16)
            scores = []
            for load in pieces:
                scores.append(lax.dot_general(q, load(0), (((1,), (1,)), ((), ())), preferred_element_type=F32))
            for s, load in zip(scores, pieces):
                top = s[:, :128]
                for t in range(1, 16):
                    top = jnp.maximum(top, s[:, t * 128:(t + 1) * 128])
                new = jnp.maximum(m, jnp.max(top, axis=1, keepdims=True))
                shrink = jnp.exp2((m - new) * scale)
                weights = jnp.exp2(s * scale - new * scale).astype(BF16)
                total = total * shrink + jnp.dot(
                    weights, jnp.concatenate([load(1), ones], axis=1), preferred_element_type=F32)
                m = new
            stat[unit, at, 0:1] = m
            stat[unit, at, 1:2] = total[:, 128:129]
            acc[unit, at, :] = total[:, :128]
            return carry
        lax.fori_loop(halves[0], halves[1], half, 0)

    def pair(first, side):
        return lambda i: kv[first:first + 2, side, i].reshape(2048, 128)

    def extra(i):
        return ext[:, i].reshape(2048, 128)

    def chunk(first, o):
        side = place(o, xl)
        return [pair(first, side), pair(first + 2, side)]

    own_a, own_1, far_a = xl, 1 - xl, 2

    def finish(j):
        at = slice(512 * j, 512 * j + 512)
        qbuf[:, at] = (acc[:, at] / stat[:, at, 1:2]).astype(BF16)
        for copy in att_sends(j):
            copy.start()

    def product(j, n):
        left = jnp.concatenate([abuf[j, zz, h] for zz in range(4) for h in range(3)], axis=1)
        return jnp.dot(left, wbuf[:, pl.ds(pl.multiple_of(n * TILE, TILE), TILE)], preferred_element_type=F32)

    def part_send(n):
        return remote(psend.at[n], prec.at[n], p_ss.at[n], p_rs.at[n],
                      {"patch": p, "head": z * 2 + 1 - xh})

    fresh_start(0)
    fresh_start(2)
    sends = [own_sends(0), own_sends(1)]
    sends[0][3].start()
    sends[1][3].start()
    for copy in sends[0][:3]:
        copy.start()
    fresh_start(1)
    fresh_start(3)
    for copy in sends[1][:3]:
        copy.start()
    own_stale.start()
    own_weight.start()
    residual.start()
    acc[...] = jnp.zeros_like(acc)
    stat[:, :, 0:1] = jnp.full((3, 1024, 1), -1e30, F32)
    stat[:, :, 1:2] = jnp.zeros((3, 1024, 1), F32)

    def pumps(*which):
        for slot, o in which:
            pump(slot, o)

    def twins(o, *slots):
        for slot in slots:
            arrived(TWIN[slot], o)

    def w_start(n):
        for copy in w_own(n):
            copy.start()

    def w_pumps(n):
        w_pump(0, n)
        w_pump(1, n)

    def give(n, carry):
        psend[n] = product(0, n).astype(BF16)
        part_send(n).start()
        return carry

    def give_chunk(n):
        w_pump(2, n)
        w_twins(n)
        lax.fori_loop(n * TILES // CHUNKS, (n + 1) * TILES // CHUNKS, give, 0)

    fresh_arrived(0)
    fresh_arrived(2)
    pumps((UP1, 0), (DN1, 0))
    w_start(0)
    twins(0, UP1, DN1)
    attend(own_a, chunk(FIRST, 0))
    pumps((XN, 0))
    w_start(1)
    attend(far_a, chunk(FIRST, 0))
    pumps((UP1, 1), (DN1, 1))
    twins(1, UP1, DN1)
    attend(own_1, chunk(FIRST, 1))
    pumps((XN, 1), (UP2, 0))
    w_start(2)

    arrived(SIB, 0)
    twins(0, XN, UP2)
    attend(own_a, chunk(SECOND, 0))
    pumps((UP2, 1))
    w_start(3)
    attend(far_a, chunk(SECOND, 0))
    pumps((XUP1, 0), (XDN1, 0))
    w_pumps(0)
    arrived(SIB, 1)
    twins(1, XN, UP2)
    attend(own_1, chunk(SECOND, 1))

    twins(0, XUP1, XDN1)
    attend(own_a, chunk(THIRD, 0))
    pumps((XUP1, 1), (XDN1, 1))
    attend(far_a, chunk(THIRD, 0))
    pumps((XUP2, 0))
    w_pumps(1)
    twins(1, XUP1, XDN1)
    attend(own_1, chunk(THIRD, 1))

    pumps((XUP2, 1))
    w_pumps(2)
    fresh_arrived(1)
    next_cache.start()
    fresh_arrived(3)
    far_cache.start()
    own_stale.wait()
    twins(0, XUP2)
    far_pieces = [extra, pair(XUP2, xl)]
    attend(own_a, chunk(LAST, 0), (0, 1))
    attend(far_a, far_pieces, (0, 1))
    twins(1, XUP2)
    attend(own_1, chunk(LAST, 1), (0, 1))
    finish(0)
    w_pumps(3)
    own_weight.wait()
    attend(own_a, chunk(LAST, 0), (1, 2))
    attend(far_a, far_pieces, (1, 2))
    att_arrived(0)
    give_chunk(0)
    attend(own_1, chunk(LAST, 1), (1, 2))
    finish(1)
    for n in range(1, CHUNKS):
        give_chunk(n)
    residual.wait()
    att_arrived(1)

    def take(n, carry):
        mine = product(1, n)
        part_send(n).wait_recv()
        cols = pl.ds(pl.multiple_of(n * TILE, TILE), TILE)
        summed = mine + prec[n].astype(F32)
        res[:, cols] = (res[:, cols].astype(F32) + gate[:, cols] * summed).astype(BF16)
        return carry
    lax.fori_loop(0, TILES, take, 0)

    result = pltpu.make_async_copy(res, out, loc.at[11])
    result.start()

    result.wait()
    next_cache.wait()
    far_cache.wait()
    for kind in range(4):
        for k in range(8):
            if k > 0 or kind > 1:
                fresh_send(kind, k).wait_send()
    for o in range(2):
        for copy in own_sends(o):
            copy.wait_send()
        for slot in TWIN:
            for copy in slot_sends(slot, o):
                copy.wait_send()
    for n in range(CHUNKS):
        for copy in w_own(n):
            copy.wait_send()
        for i in range(3):
            for copy in w_sends(i, n):
                copy.wait_send()
    for j in range(2):
        for copy in att_sends(j)[1:]:
            copy.wait_send()

    def sent(n, carry):
        part_send(n).wait_send()
        return carry
    lax.fori_loop(0, TILES, sent, 0)


def block(fresh, stale, weight, stream, gate):
    any_ = pl.BlockSpec(memory_space=pl.ANY)
    vmem = pl.BlockSpec(memory_space=pltpu.VMEM)
    dma = pltpu.SemaphoreType.DMA
    return pl.pallas_call(
        block_kernel,
        out_shape=[jax.ShapeDtypeStruct((128, 5120), BF16),
                   jax.ShapeDtypeStruct((3, 2, 1024, 128), BF16)],
        in_specs=[any_, any_, any_, any_, vmem],
        out_specs=[any_, any_],
        scratch_shapes=[
            pltpu.VMEM((16, 2, 2, 1024, 128), BF16),
            pltpu.VMEM((2, 2, 1024, 128), BF16),
            pltpu.VMEM((3, 1024, 128), BF16),
            pltpu.VMEM((3, 1024, 128), F32),
            pltpu.VMEM((3, 1024, 2), F32),
            pltpu.VMEM((1536, 5120), BF16),
            pltpu.VMEM((2, 4, 3, 128, 128), BF16),
            pltpu.VMEM((128, 5120), BF16),
            pltpu.VMEM((TILES, 128, TILE), BF16),
            pltpu.VMEM((TILES, 128, TILE), BF16),
            dma((N_SENDS, 2)), dma((16, 2)),
            dma((4, 8)), dma((4, 8)),
            dma((6, CHUNKS)), dma((6, CHUNKS)),
            dma((2, 2, 4)), dma((2, 2, 4)),
            dma((TILES,)), dma((TILES,)),
            dma((12,)),
        ],
        compiler_params=pltpu.CompilerParams(
            collective_id=0, has_side_effects=True, vmem_limit_bytes=62 * 2**20),
        name="gather_attend",
    )(fresh, stale, weight, stream, gate)


def per_device(fresh_qkv, stale_cache, out_weight, stream, gate_scale):
    fresh = jnp.transpose(fresh_qkv.reshape(128, 3, 8, 3, 128), (2, 3, 1, 0, 4))
    stale = jnp.transpose(stale_cache, (2, 1, 0, 3))
    block_out, cache = block(fresh, stale, out_weight, stream, gate_scale.reshape(1, -1))
    return (block_out, jnp.transpose(cache, (2, 1, 0, 3)))


def solution(mesh):
    return jax.shard_map(
        per_device,
        mesh=mesh,
        in_specs=(
            P(("patch", "head"), None, None, None),
            P("patch", None, "head", None),
            P("head", None),
            P(("patch", "head"), None),
            P(),
        ),
        out_specs=(P(("patch", "head"), None), P("patch", None, "head", None)),
        check_vma=False,
    )
```

```python
import functools
import math

import jax
import jax.numpy as jnp
from jax import lax
from jax.experimental import pallas as pl
from jax.experimental.pallas import tpu as pltpu
from jax.sharding import PartitionSpec as P

MESH = pl.DeviceIdType.MESH
BF16 = jnp.bfloat16
F32 = jnp.float32

SIB, UP2, UP1, DN1, XDN1, XUP1, OWN, XN, XUP2 = 0, 2, 4, 5, 8, 10, 12, 13, 14
TWIN = {XN: 1, UP2: 3, UP1: 6, DN1: 7, XDN1: 9, XUP1: 11, XUP2: 15}
FIRST, SECOND, THIRD, LAST = 4, 0, 8, 12
KINDS = ["own_sib", "own_dn", "own_up", "own_x", "up1_dn", "xn_dn", "xn_up", "xup1_dn", "dn1_x"]
SEND = {name: i for i, name in enumerate(KINDS)}
SIB_SEND = {slot: len(KINDS) + i for i, slot in enumerate(TWIN)}
N_SENDS = len(KINDS) + len(TWIN)
TILES, TILE = 8, 640
CHUNKS, HALF = 4, 2560


def block_kernel(fresh, stale, weight, stream, gate, out, cache_out,
                 kv, ext, qbuf, acc, stat, wbuf, abuf, res, psend, prec,
                 kv_ss, kv_rs, in_ss, in_rs, w_ss, w_rs, x_ss, x_rs, a_ss, a_rs, p_ss, p_rs, loc):
    rows = 128
    p = lax.axis_index("patch")
    g = lax.axis_index("head")
    y, xl, c = p // 4, (p // 2) % 2, p % 2
    z, xh = g // 2, g % 2
    fwd = 1 + 2 * c
    xp = (y * 2 + 1 - xl) * 2 + c

    def patch_dev(yy, xx, cc):
        return {"patch": (yy * 2 + xx) * 2 + cc, "head": g}

    sib = patch_dev(y, xl, 1 - c)
    dn = patch_dev((y + fwd) % 4, xl, c)
    up = patch_dev((y + 4 - fwd) % 4, xl, c)
    xn = patch_dev(y, 1 - xl, c)

    def head_dev(patch, k):
        return {"patch": patch, "head": (g + k) % 8}

    def z_dev(patch, k):
        return {"patch": patch, "head": ((z + k) % 4) * 2 + xh}

    def signal(dev):
        pl.semaphore_signal(barrier, inc=1, device_id=dev, device_id_type=MESH)

    barrier = pltpu.get_barrier_semaphore()
    for dev in (sib, dn, up, xn):
        signal(dev)
    for k in range(1, 8):
        signal(head_dev(p, k))
        signal(head_dev(xp, k))
    pl.semaphore_wait(barrier, 18)

    def remote(src, dst, ss, rs, dev):
        return pltpu.make_async_remote_copy(
            src_ref=src, dst_ref=dst, send_sem=ss, recv_sem=rs, device_id=dev, device_id_type=MESH)

    far_head = 2 - 2 * xl
    tokens = pl.ds(pl.multiple_of(g * rows, rows), rows)

    def fresh_send(kind, k):
        to = (g + k) % 8
        near = pl.ds(xl, 2)
        if kind == 0:
            src, dst, patch = fresh.at[to, near, 0], qbuf.at[0:2, tokens], p
        elif kind == 1:
            src, dst, patch = fresh.at[to, near, 1:3], kv.at[OWN, :, :, tokens], p
        elif kind == 2:
            src, dst, patch = fresh.at[to, far_head, 0], qbuf.at[2, tokens], xp
        else:
            src, dst, patch = fresh.at[to, far_head, 1:3], ext.at[1, :, tokens], xp
        if patch is p and k == 0:
            return pltpu.make_async_copy(src, dst, loc.at[kind])
        return remote(src, dst, in_ss.at[kind, k], in_rs.at[kind, k], head_dev(patch, k))

    def fresh_start(kind):
        for k in range(8):
            fresh_send(kind, k).start()

    def fresh_arrived(kind):
        for k in range(8):
            if k == 0 and kind < 2:
                fresh_send(kind, k).wait()
            else:
                fresh_send(kind, k).wait_recv()

    def place(o, side):
        return side if o == 0 else 1 - side

    def block_send(kind, src, slot, o, side, dev):
        return remote(src, kv.at[slot, place(o, side)], kv_ss.at[kind, o], kv_rs.at[slot, o], dev)

    def own_sends(o):
        near = stale.at[2 * xl if o == 0 else 1]
        far = stale.at[far_head if o == 0 else 1]
        return [block_send(SEND["own_dn"], near, UP1, o, xl, dn),
                block_send(SEND["own_up"], near, DN1, o, xl, up),
                block_send(SEND["own_sib"], near, SIB, o, xl, sib),
                block_send(SEND["own_x"], far, XN, o, 1 - xl, xn)]

    routes = [{UP1: [("up1_dn", UP2, xl, dn)], XUP1: [("xup1_dn", XUP2, xl, dn)],
               XN: [("xn_dn", XUP1, xl, dn), ("xn_up", XDN1, xl, up)]},
              {UP1: [("up1_dn", UP2, xl, dn)], XUP1: [("xup1_dn", XUP2, xl, dn)],
               XN: [("xn_dn", XUP1, xl, dn)], DN1: [("dn1_x", XDN1, 1 - xl, xn)]}]

    def arrived(slot, o):
        here = kv.at[slot, place(o, xl)]
        remote(here, here, kv_ss.at[0, o], kv_rs.at[slot, o], sib).wait_recv()

    def slot_sends(slot, o):
        here = kv.at[slot, place(o, xl)]
        out_ = [block_send(SEND[name], here, target, o, side, dev)
                for name, target, side, dev in routes[o].get(slot, [])]
        return out_ + [block_send(SIB_SEND[slot], here, TWIN[slot], o, xl, sib)]

    def pump(slot, o):
        arrived(slot, o)
        for copy in slot_sends(slot, o):
            copy.start()

    eq = 1 - (xh + xl) % 2
    odd = {"patch": xp, "head": z * 2 + 1 - xh}

    def w_cols(core, n):
        return pl.ds(pl.multiple_of(core * HALF + n * TILE, TILE), TILE)

    def w_head(head):
        return pl.ds(pl.multiple_of(head * rows, rows), rows)

    def w_slot(slot):
        return pl.ds(pl.multiple_of(z * 384 + slot * rows, rows), rows)

    def w_local(i, n):
        head, slot = (eq * xl + (1 - eq) * 2 * xl, (1 - eq) * 2) if i == 0 else (xl + 1, 1)
        return pltpu.make_async_copy(
            weight.at[w_head(head), w_cols(c, n)], wbuf.at[w_slot(slot), w_cols(c, n)], x_ss.at[2 + i, n])

    def w_cross(i, n):
        head, slot = (eq * far_head + (1 - eq) * (1 - xl), eq * 2) if i == 0 else (2 - xl, 1)
        return remote(weight.at[w_head(head), w_cols(c, n)], wbuf.at[w_slot(slot), w_cols(c, n)],
                      x_ss.at[i, n], x_rs.at[i, n], odd)

    def w_fetch(n):
        w_local(0, n).start()
        w_cross(0, n).start()

        @pl.when(eq == 1)
        def _():
            w_local(1, n).start()

        @pl.when(eq == 0)
        def _():
            w_cross(1, n).start()

    def w_fetched(n):
        w_local(0, n).wait()
        w_cross(0, n).wait()

        @pl.when(eq == 1)
        def _():
            w_local(1, n).wait()

        @pl.when(eq == 0)
        def _():
            w_cross(1, n).wait()

    def w_at(origin, core, n):
        return pl.ds(pl.multiple_of(((z + origin) % 4) * 384, 384), 384), w_cols(core, n)

    def w_own(n):
        here = wbuf.at[w_at(0, c, n)]
        return [remote(here, here, w_ss.at[0, n], w_rs.at[0, n], z_dev(p, fwd)),
                remote(here, here, w_ss.at[1, n], w_rs.at[1, n], z_dev(p, 4 - fwd)),
                remote(here, here, w_ss.at[6, n], w_rs.at[6, n], sib)]

    def w_origin(i):
        return (4 - fwd, fwd, 2)[i]

    def w_sends(i, n):
        here = wbuf.at[w_at(w_origin(i), c, n)]
        copies = [remote(here, here, w_ss.at[2 + i, n], w_rs.at[3 + i, n], sib)]
        if i == 0:
            copies.insert(0, remote(here, here, w_ss.at[5, n], w_rs.at[2, n], z_dev(p, fwd)))
        return copies

    def w_pump(i, n):
        here = wbuf.at[w_at(w_origin(i), c, n)]
        remote(here, here, w_ss.at[0, n], w_rs.at[i, n], sib).wait_recv()
        for copy in w_sends(i, n):
            copy.start()

    def w_twins(n):
        for i in range(4):
            origin = (fwd, 4 - fwd, 2, 0)[i]
            here = wbuf.at[w_at(origin, 1 - c, n)]
            remote(here, here, w_ss.at[0, n], w_rs.at[3 + i, n], sib).wait_recv()

    own_stale = pltpu.make_async_copy(stale.at[2 * xl], ext.at[0], loc.at[6])
    residual = pltpu.make_async_copy(stream, res, loc.at[7])
    next_cache = pltpu.make_async_copy(kv.at[OWN], cache_out.at[pl.ds(xl, 2)], loc.at[8])

    far_cache = remote(ext.at[1], cache_out.at[2 * xl], loc.at[2], loc.at[3], xn)

    def att_send(unit, k, piece):
        to = (g + k) % 8
        lead = eq * xl + (1 - eq) * 2
        if unit == 0:
            src_block, patch, kind, slot, which = to, p, 1, lead, xl
        elif unit == 2:
            src_block, patch, kind, slot, which = (to if piece == 0 else to + 1 - 2 * (to % 2)), p, 0, lead, 2
        else:
            src_block = to if piece == 0 else to + (1 - eq) * (1 - 2 * (to % 2))
            patch, kind, slot, which = eq * p + (1 - eq) * xp, eq, eq * (1 - xl) + (1 - eq) * xl, 1 - xl
        src = qbuf.at[which, pl.ds(pl.multiple_of(src_block * rows + 64 * piece, 64), 64)]
        dst = abuf.at[kind, z, slot, pl.ds(64 * piece, 64)]
        arrival = a_rs.at[kind, z, slot, piece]
        near = pltpu.make_async_copy(src, dst, arrival)
        far = remote(src, dst, a_ss.at[unit, k, piece], arrival, {"patch": patch, "head": to})
        return near, far

    def att_each(use_near, use_far, unit):
        for k in range(8):
            for piece in range(2):
                near, far = att_send(unit, k, piece)
                if k > 0:
                    use_far(far)
                elif unit != 1:
                    use_near(near)
                else:
                    @pl.when(eq == 1)
                    def _(near=near):
                        use_near(near)

                    @pl.when(eq == 0)
                    def _(far=far):
                        use_far(far)

    def att_arrived(kind):
        for zz in range(4):
            for slot in range(3):
                for piece in range(2):
                    here = abuf.at[kind, zz, slot, pl.ds(64 * piece, 64)]
                    remote(here, here, a_ss.at[0, 1, 0], a_rs.at[kind, zz, slot, piece], sib).wait_recv()

    scale = math.log2(math.e) / math.sqrt(128)

    def scores_of(unit, at, load):
        return lax.dot_general(qbuf[unit, at, :], load(0), (((1,), (1,)), ((), ())), preferred_element_type=F32)

    def fold(s, load, m, total):
        top = s[:, :128]
        for t in range(1, 16):
            top = jnp.maximum(top, s[:, t * 128:(t + 1) * 128])
        new = jnp.maximum(m, jnp.max(top, axis=1, keepdims=True))
        shrink = jnp.exp2((m - new) * scale)
        weights = jnp.exp2(s * scale - new * scale).astype(BF16)
        total = total * shrink + jnp.dot(
            weights, jnp.concatenate([load(1), jnp.ones((2048, 128), BF16)], axis=1), preferred_element_type=F32)
        return new, total

    def state(unit, at):
        return stat[unit, at, 0:1], jnp.concatenate(
            [acc[unit, at, :], jnp.broadcast_to(stat[unit, at, 1:2], (512, 128))], axis=1)

    def keep(unit, at, m, total):
        stat[unit, at, 0:1] = m
        stat[unit, at, 1:2] = total[:, 128:129]
        acc[unit, at, :] = total[:, :128]

    def attend(unit, pieces, halves=(0, 2)):
        def half(j, carry):
            at = pl.ds(pl.multiple_of(j * 512, 512), 512)
            now = state(unit, at)
            scores = [scores_of(unit, at, load) for load in pieces]
            for s, load in zip(scores, pieces):
                now = fold(s, load, *now)
            keep(unit, at, *now)
            return carry
        lax.fori_loop(halves[0], halves[1], half, 0)

    def attend_piece(unit, load):
        halves = [pl.ds(0, 512), pl.ds(512, 512)]
        scores = [scores_of(unit, at, load) for at in halves]
        for s, at in zip(scores, halves):
            keep(unit, at, *fold(s, load, *state(unit, at)))

    def pair(first, side):
        return lambda i: kv[first:first + 2, side, i].reshape(2048, 128)

    def extra(i):
        return ext[:, i].reshape(2048, 128)

    def chunk(first, o):
        side = place(o, xl)
        return [pair(first, side), pair(first + 2, side)]

    own_a, own_1, far_a = xl, 1 - xl, 2

    def finish(unit):
        which = (xl, 1 - xl, 2)[unit]
        qbuf[which] = (acc[which] / stat[which, :, 1:2]).astype(BF16)
        att_each(lambda copy: copy.start(), lambda copy: copy.start(), unit)

    def product(j, n):
        left = jnp.concatenate([abuf[j, zz, h] for zz in range(4) for h in range(3)], axis=1)
        return jnp.dot(left, wbuf[:, pl.ds(pl.multiple_of(n * TILE, TILE), TILE)], preferred_element_type=F32)

    def part_sends(n):
        return [remote(psend.at[n, pl.ds(64 * i, 64)], prec.at[n, pl.ds(64 * i, 64)],
                       p_ss.at[i, n], p_rs.at[i, n], (xn, odd)[i]) for i in range(2)]

    fresh_start(0)
    fresh_start(2)
    sends = [own_sends(0), own_sends(1)]
    sends[0][3].start()
    sends[1][3].start()
    for copy in sends[0][:3]:
        copy.start()
    for copy in sends[1][:3]:
        copy.start()
    for n in range(CHUNKS):
        w_fetch(n)
    own_stale.start()
    residual.start()
    acc[...] = jnp.zeros_like(acc)
    stat[:, :, 0:1] = jnp.full((3, 1024, 1), -1e30, F32)
    stat[:, :, 1:2] = jnp.zeros((3, 1024, 1), F32)

    def pumps(*which):
        for slot, o in which:
            pump(slot, o)

    def twins(o, *slots):
        for slot in slots:
            arrived(TWIN[slot], o)

    def w_start(n):
        w_fetched(n)
        for copy in w_own(n):
            copy.start()

    def w_pumps(n):
        w_pump(0, n)
        w_pump(1, n)

    def give(n, carry):
        psend[n] = product(0, n).astype(BF16)
        for copy in part_sends(n):
            copy.start()
        return carry

    def give_chunk(n):
        w_pump(2, n)
        w_twins(n)
        lax.fori_loop(0, 2, lambda i, carry: give(n + CHUNKS * i, carry), 0)

    fresh_arrived(0)
    fresh_arrived(2)
    pumps((UP1, 0), (DN1, 0))
    fresh_start(1)
    fresh_start(3)
    w_start(0)
    twins(0, UP1, DN1)
    attend(own_a, chunk(FIRST, 0))
    pumps((XN, 0))
    w_start(1)
    attend(far_a, chunk(FIRST, 0))
    pumps((UP1, 1), (DN1, 1))
    twins(1, UP1, DN1)
    attend(own_1, chunk(FIRST, 1))
    pumps((XN, 1), (UP2, 0))
    w_start(2)

    arrived(SIB, 0)
    twins(0, XN, UP2)
    attend(own_a, chunk(SECOND, 0))
    pumps((UP2, 1))
    w_start(3)
    attend(far_a, chunk(SECOND, 0))
    pumps((XUP1, 0), (XDN1, 0))
    w_pumps(0)
    arrived(SIB, 1)
    twins(1, XN, UP2)
    attend(own_1, chunk(SECOND, 1))

    twins(0, XUP1, XDN1)
    attend(far_a, chunk(THIRD, 0))
    pumps((XUP1, 1), (XDN1, 1))
    attend(own_a, chunk(THIRD, 0))
    w_pumps(1)
    twins(1, XUP1, XDN1)
    attend(own_1, chunk(THIRD, 1))

    pumps((XUP2, 0))
    fresh_arrived(3)
    far_cache.start()
    own_stale.wait()
    attend_piece(far_a, extra)
    pumps((XUP2, 1))
    w_pumps(2)
    fresh_arrived(1)
    next_cache.start()
    attend_piece(own_1, pair(OWN, 1 - xl))
    attend_piece(own_a, pair(OWN, xl))

    twins(0, XUP2)
    attend_piece(far_a, pair(XUP2, xl))
    finish(2)
    twins(1, XUP2)
    attend_piece(own_1, pair(XUP2, 1 - xl))
    finish(1)
    w_pumps(3)
    attend_piece(own_a, pair(XUP2, xl))
    finish(0)
    att_arrived(0)
    give_chunk(0)
    for n in range(1, CHUNKS):
        give_chunk(n)
    residual.wait()
    att_arrived(1)

    def take(n, carry):
        mine = product(1, n)
        for copy in part_sends(n):
            copy.wait_recv()
        cols = pl.ds(pl.multiple_of(n * TILE, TILE), TILE)
        summed = mine + prec[n].astype(F32)
        res[:, cols] = (res[:, cols].astype(F32) + gate[:, cols] * summed).astype(BF16)
        return carry
    lax.fori_loop(0, TILES, take, 0)

    result = pltpu.make_async_copy(res, out, loc.at[11])
    result.start()

    result.wait()
    next_cache.wait()
    far_cache.wait()
    for kind in range(4):
        for k in range(8):
            if k > 0 or kind > 1:
                fresh_send(kind, k).wait_send()
    for o in range(2):
        for copy in own_sends(o):
            copy.wait_send()
        for slot in TWIN:
            for copy in slot_sends(slot, o):
                copy.wait_send()
    for n in range(CHUNKS):
        for copy in w_own(n):
            copy.wait_send()
        for i in range(3):
            for copy in w_sends(i, n):
                copy.wait_send()
    for unit in range(3):
        att_each(lambda copy: None, lambda copy: copy.wait_send(), unit)

    def sent(n, carry):
        for copy in part_sends(n):
            copy.wait_send()
        return carry
    lax.fori_loop(0, TILES, sent, 0)


def block(fresh, stale, weight, stream, gate):
    any_ = pl.BlockSpec(memory_space=pl.ANY)
    vmem = pl.BlockSpec(memory_space=pltpu.VMEM)
    dma = pltpu.SemaphoreType.DMA
    return pl.pallas_call(
        block_kernel,
        out_shape=[jax.ShapeDtypeStruct((128, 5120), BF16),
                   jax.ShapeDtypeStruct((3, 2, 1024, 128), BF16)],
        in_specs=[any_, any_, any_, any_, vmem],
        out_specs=[any_, any_],
        scratch_shapes=[
            pltpu.VMEM((16, 2, 2, 1024, 128), BF16),
            pltpu.VMEM((2, 2, 1024, 128), BF16),
            pltpu.VMEM((3, 1024, 128), BF16),
            pltpu.VMEM((3, 1024, 128), F32),
            pltpu.VMEM((3, 1024, 2), F32),
            pltpu.VMEM((1536, 5120), BF16),
            pltpu.VMEM((2, 4, 3, 128, 128), BF16),
            pltpu.VMEM((128, 5120), BF16),
            pltpu.VMEM((TILES, 128, TILE), BF16),
            pltpu.VMEM((TILES, 128, TILE), BF16),
            dma((N_SENDS, 2)), dma((16, 2)),
            dma((4, 8)), dma((4, 8)),
            dma((7, CHUNKS)), dma((7, CHUNKS)),
            dma((4, CHUNKS)), dma((2, CHUNKS)),
            dma((3, 8, 2)), dma((2, 4, 3, 2)),
            dma((2, TILES)), dma((2, TILES)),
            dma((12,)),
        ],
        compiler_params=pltpu.CompilerParams(
            collective_id=0, has_side_effects=True, vmem_limit_bytes=62 * 2**20),
        name="gather_attend",
    )(fresh, stale, weight, stream, gate)


def per_device(fresh_qkv, stale_cache, out_weight, stream, gate_scale):
    fresh = jnp.transpose(fresh_qkv.reshape(128, 3, 8, 3, 128), (2, 3, 1, 0, 4))
    stale = jnp.transpose(stale_cache, (2, 1, 0, 3))
    block_out, cache = block(fresh, stale, out_weight, stream, gate_scale.reshape(1, -1))
    return (block_out, jnp.transpose(cache, (2, 1, 0, 3)))


def solution(mesh):
    return jax.shard_map(
        per_device,
        mesh=mesh,
        in_specs=(
            P(("patch", "head"), None, None, None),
            P("patch", None, "head", None),
            P("head", None),
            P(("patch", "head"), None),
            P(),
        ),
        out_specs=(P(("patch", "head"), None), P("patch", None, "head", None)),
        check_vma=False,
    )
```

```python
import functools
import math

import jax
import jax.numpy as jnp
from jax import lax
from jax.experimental import pallas as pl
from jax.experimental.pallas import tpu as pltpu
from jax.sharding import PartitionSpec as P

MESH = pl.DeviceIdType.MESH
BF16 = jnp.bfloat16
F32 = jnp.float32

SIB, UP2, UP1, DN1, XDN1, XUP1, OWN, XN, XUP2 = 0, 2, 4, 5, 8, 10, 12, 13, 14
TWIN = {XN: 1, UP2: 3, UP1: 6, DN1: 7, XDN1: 9, XUP1: 11, XUP2: 15}
FIRST, SECOND, THIRD, LAST = 4, 0, 8, 12
KINDS = ["own_sib", "own_dn", "own_up", "own_x", "up1_dn", "xn_dn", "xn_up", "xup1_dn", "dn1_x"]
SEND = {name: i for i, name in enumerate(KINDS)}
SIB_SEND = {slot: len(KINDS) + i for i, slot in enumerate(TWIN)}
N_SENDS = len(KINDS) + len(TWIN)
TILES, TILE = 8, 640
CHUNKS, HALF = 4, 2560


def block_kernel(fresh, stale, weight, stream, gate, out, cache_out,
                 kv, ext, qbuf, acc, stat, wbuf, abuf, res, psend, prec,
                 kv_ss, kv_rs, in_ss, in_rs, w_ss, w_rs, x_ss, x_rs, a_ss, a_rs, p_ss, p_rs, loc):
    rows = 128
    p = lax.axis_index("patch")
    g = lax.axis_index("head")
    y, xl, c = p // 4, (p // 2) % 2, p % 2
    z, xh = g // 2, g % 2
    fwd = 1 + 2 * c
    xp = (y * 2 + 1 - xl) * 2 + c

    def patch_dev(yy, xx, cc):
        return {"patch": (yy * 2 + xx) * 2 + cc, "head": g}

    sib = patch_dev(y, xl, 1 - c)
    dn = patch_dev((y + fwd) % 4, xl, c)
    up = patch_dev((y + 4 - fwd) % 4, xl, c)
    xn = patch_dev(y, 1 - xl, c)

    def head_dev(patch, k):
        return {"patch": patch, "head": (g + k) % 8}

    def z_dev(patch, k):
        return {"patch": patch, "head": ((z + k) % 4) * 2 + xh}

    def signal(dev):
        pl.semaphore_signal(barrier, inc=1, device_id=dev, device_id_type=MESH)

    barrier = pltpu.get_barrier_semaphore()
    for dev in (sib, dn, up, xn):
        signal(dev)
    for k in range(1, 8):
        signal(head_dev(p, k))
        signal(head_dev(xp, k))
    pl.semaphore_wait(barrier, 18)

    def remote(src, dst, ss, rs, dev):
        return pltpu.make_async_remote_copy(
            src_ref=src, dst_ref=dst, send_sem=ss, recv_sem=rs, device_id=dev, device_id_type=MESH)

    far_head = 2 - 2 * xl
    tokens = pl.ds(pl.multiple_of(g * rows, rows), rows)

    def fresh_send(kind, k):
        to = (g + k) % 8
        near = pl.ds(xl, 2)
        if kind == 0:
            src, dst, patch = fresh.at[to, near, 0], qbuf.at[0:2, tokens], p
        elif kind == 1:
            src, dst, patch = fresh.at[to, near, 1:3], kv.at[OWN, :, :, tokens], p
        elif kind == 2:
            src, dst, patch = fresh.at[to, far_head, 0], qbuf.at[2, tokens], xp
        else:
            src, dst, patch = fresh.at[to, far_head, 1:3], ext.at[1, :, tokens], xp
        if patch is p and k == 0:
            return pltpu.make_async_copy(src, dst, loc.at[kind])
        return remote(src, dst, in_ss.at[kind, k], in_rs.at[kind, k], head_dev(patch, k))

    def fresh_start(kind):
        for k in range(8):
            fresh_send(kind, k).start()

    def fresh_arrived(kind):
        for k in range(8):
            if k == 0 and kind < 2:
                fresh_send(kind, k).wait()
            else:
                fresh_send(kind, k).wait_recv()

    def place(o, side):
        return side if o == 0 else 1 - side

    def block_send(kind, src, slot, o, side, dev):
        return remote(src, kv.at[slot, place(o, side)], kv_ss.at[kind, o], kv_rs.at[slot, o], dev)

    def own_sends(o):
        near = stale.at[2 * xl if o == 0 else 1]
        far = stale.at[far_head if o == 0 else 1]
        return [block_send(SEND["own_dn"], near, UP1, o, xl, dn),
                block_send(SEND["own_up"], near, DN1, o, xl, up),
                block_send(SEND["own_sib"], near, SIB, o, xl, sib),
                block_send(SEND["own_x"], far, XN, o, 1 - xl, xn)]

    routes = [{UP1: [("up1_dn", UP2, xl, dn)], XUP1: [("xup1_dn", XUP2, xl, dn)],
               XN: [("xn_dn", XUP1, xl, dn), ("xn_up", XDN1, xl, up)]},
              {UP1: [("up1_dn", UP2, xl, dn)], XUP1: [("xup1_dn", XUP2, xl, dn)],
               XN: [("xn_dn", XUP1, xl, dn)], DN1: [("dn1_x", XDN1, 1 - xl, xn)]}]

    def arrived(slot, o):
        here = kv.at[slot, place(o, xl)]
        remote(here, here, kv_ss.at[0, o], kv_rs.at[slot, o], sib).wait_recv()

    def slot_sends(slot, o):
        here = kv.at[slot, place(o, xl)]
        out_ = [block_send(SEND[name], here, target, o, side, dev)
                for name, target, side, dev in routes[o].get(slot, [])]
        return out_ + [block_send(SIB_SEND[slot], here, TWIN[slot], o, xl, sib)]

    def pump(slot, o):
        arrived(slot, o)
        for copy in slot_sends(slot, o):
            copy.start()

    eq = 1 - (xh + xl) % 2
    odd = {"patch": xp, "head": z * 2 + 1 - xh}

    def w_cols(core, n):
        return pl.ds(pl.multiple_of(core * HALF + n * TILE, TILE), TILE)

    def w_head(head):
        return pl.ds(pl.multiple_of(head * rows, rows), rows)

    def w_slot(slot):
        return pl.ds(pl.multiple_of(z * 384 + slot * rows, rows), rows)

    def w_local(i, n):
        head, slot = (eq * xl + (1 - eq) * 2 * xl, (1 - eq) * 2) if i == 0 else (xl + 1, 1)
        return pltpu.make_async_copy(
            weight.at[w_head(head), w_cols(c, n)], wbuf.at[w_slot(slot), w_cols(c, n)], x_ss.at[2 + i, n])

    def w_cross(i, n):
        head, slot = (eq * far_head + (1 - eq) * (1 - xl), eq * 2) if i == 0 else (2 - xl, 1)
        return remote(weight.at[w_head(head), w_cols(c, n)], wbuf.at[w_slot(slot), w_cols(c, n)],
                      x_ss.at[i, n], x_rs.at[i, n], odd)

    def w_fetch(n):
        w_local(0, n).start()
        w_cross(0, n).start()

        @pl.when(eq == 1)
        def _():
            w_local(1, n).start()

        @pl.when(eq == 0)
        def _():
            w_cross(1, n).start()

    def w_fetched(n):
        w_local(0, n).wait()
        w_cross(0, n).wait()

        @pl.when(eq == 1)
        def _():
            w_local(1, n).wait()

        @pl.when(eq == 0)
        def _():
            w_cross(1, n).wait()

    def w_at(origin, core, n):
        return pl.ds(pl.multiple_of(((z + origin) % 4) * 384, 384), 384), w_cols(core, n)

    def w_own(n):
        here = wbuf.at[w_at(0, c, n)]
        return [remote(here, here, w_ss.at[0, n], w_rs.at[0, n], z_dev(p, fwd)),
                remote(here, here, w_ss.at[1, n], w_rs.at[1, n], z_dev(p, 4 - fwd)),
                remote(here, here, w_ss.at[6, n], w_rs.at[6, n], sib)]

    def w_origin(i):
        return (4 - fwd, fwd, 2)[i]

    def w_sends(i, n):
        here = wbuf.at[w_at(w_origin(i), c, n)]
        copies = [remote(here, here, w_ss.at[2 + i, n], w_rs.at[3 + i, n], sib)]
        if i == 0:
            copies.insert(0, remote(here, here, w_ss.at[5, n], w_rs.at[2, n], z_dev(p, fwd)))
        return copies

    def w_pump(i, n):
        here = wbuf.at[w_at(w_origin(i), c, n)]
        remote(here, here, w_ss.at[0, n], w_rs.at[i, n], sib).wait_recv()
        for copy in w_sends(i, n):
            copy.start()

    def w_twins(n):
        for i in range(4):
            origin = (fwd, 4 - fwd, 2, 0)[i]
            here = wbuf.at[w_at(origin, 1 - c, n)]
            remote(here, here, w_ss.at[0, n], w_rs.at[3 + i, n], sib).wait_recv()

    own_stale = pltpu.make_async_copy(stale.at[2 * xl], ext.at[0], loc.at[6])
    residual = pltpu.make_async_copy(stream, res, loc.at[7])
    next_cache = pltpu.make_async_copy(kv.at[OWN], cache_out.at[pl.ds(xl, 2)], loc.at[8])

    far_cache = remote(ext.at[1], cache_out.at[2 * xl], loc.at[2], loc.at[3], xn)

    def att_send(unit, k, piece):
        to = (g + k) % 8
        lead = eq * xl + (1 - eq) * 2
        if unit == 0:
            src_block, patch, kind, slot, which = to, p, 1, lead, xl
        elif unit == 2:
            src_block, patch, kind, slot, which = (to if piece == 0 else to + 1 - 2 * (to % 2)), p, 0, lead, 2
        else:
            src_block = to if piece == 0 else to + (1 - eq) * (1 - 2 * (to % 2))
            patch, kind, slot, which = eq * p + (1 - eq) * xp, eq, eq * (1 - xl) + (1 - eq) * xl, 1 - xl
        src = qbuf.at[which, pl.ds(pl.multiple_of(src_block * rows + 64 * piece, 64), 64)]
        dst = abuf.at[kind, z, slot, pl.ds(64 * piece, 64)]
        arrival = a_rs.at[kind, z, slot, piece]
        near = pltpu.make_async_copy(src, dst, arrival)
        far = remote(src, dst, a_ss.at[unit, k, piece], arrival, {"patch": patch, "head": to})
        return near, far

    def att_each(use_near, use_far, unit):
        for k in range(8):
            for piece in range(2):
                near, far = att_send(unit, k, piece)
                if k > 0:
                    use_far(far)
                elif unit != 1:
                    use_near(near)
                else:
                    @pl.when(eq == 1)
                    def _(near=near):
                        use_near(near)

                    @pl.when(eq == 0)
                    def _(far=far):
                        use_far(far)

    def att_arrived(kind):
        for zz in range(4):
            for slot in range(3):
                for piece in range(2):
                    here = abuf.at[kind, zz, slot, pl.ds(64 * piece, 64)]
                    remote(here, here, a_ss.at[0, 1, 0], a_rs.at[kind, zz, slot, piece], sib).wait_recv()

    scale = math.log2(math.e) / math.sqrt(128)

    def scores_of(unit, at, load):
        return lax.dot_general(qbuf[unit, at, :], load(0), (((1,), (1,)), ((), ())), preferred_element_type=F32)

    def fold(s, load, m, total):
        top = s[:, :128]
        for t in range(1, 16):
            top = jnp.maximum(top, s[:, t * 128:(t + 1) * 128])
        new = jnp.maximum(m, jnp.max(top, axis=1, keepdims=True))
        shrink = jnp.exp2((m - new) * scale)
        weights = jnp.exp2(s * scale - new * scale).astype(BF16)
        total = total * shrink + jnp.dot(
            weights, jnp.concatenate([load(1), jnp.ones((2048, 128), BF16)], axis=1), preferred_element_type=F32)
        return new, total

    def state(unit, at):
        return stat[unit, at, 0:1], jnp.concatenate(
            [acc[unit, at, :], jnp.broadcast_to(stat[unit, at, 1:2], (512, 128))], axis=1)

    def keep(unit, at, m, total):
        stat[unit, at, 0:1] = m
        stat[unit, at, 1:2] = total[:, 128:129]
        acc[unit, at, :] = total[:, :128]

    def attend(unit, pieces, halves=(0, 2)):
        def half(j, carry):
            at = pl.ds(pl.multiple_of(j * 512, 512), 512)
            now = state(unit, at)
            scores = [scores_of(unit, at, load) for load in pieces]
            for s, load in zip(scores, pieces):
                now = fold(s, load, *now)
            keep(unit, at, *now)
            return carry
        lax.fori_loop(halves[0], halves[1], half, 0)

    def attend_piece(unit, load):
        halves = [pl.ds(0, 512), pl.ds(512, 512)]
        scores = [scores_of(unit, at, load) for at in halves]
        for s, at in zip(scores, halves):
            keep(unit, at, *fold(s, load, *state(unit, at)))

    def pair(first, side):
        return lambda i: kv[first:first + 2, side, i].reshape(2048, 128)

    def extra(i):
        return ext[:, i].reshape(2048, 128)

    def chunk(first, o):
        side = place(o, xl)
        return [pair(first, side), pair(first + 2, side)]

    own_a, own_1, far_a = xl, 1 - xl, 2

    def finish(unit):
        which = (xl, 1 - xl, 2)[unit]
        qbuf[which] = (acc[which] / stat[which, :, 1:2]).astype(BF16)
        att_each(lambda copy: copy.start(), lambda copy: copy.start(), unit)

    def product(j, n):
        left = jnp.concatenate([abuf[j, zz, h] for zz in range(4) for h in range(3)], axis=1)
        return jnp.dot(left, wbuf[:, pl.ds(pl.multiple_of(n * TILE, TILE), TILE)], preferred_element_type=F32)

    def part_sends(n):
        return [remote(psend.at[n, pl.ds(64 * i, 64)], prec.at[n, pl.ds(64 * i, 64)],
                       p_ss.at[i, n], p_rs.at[i, n], (xn, odd)[i]) for i in range(2)]

    fresh_start(0)
    fresh_start(2)
    sends = [own_sends(0), own_sends(1)]
    sends[0][3].start()
    sends[1][3].start()
    for copy in sends[0][:3]:
        copy.start()
    for copy in sends[1][:3]:
        copy.start()
    for n in range(CHUNKS):
        w_fetch(n)
    own_stale.start()
    residual.start()
    acc[...] = jnp.zeros_like(acc)
    stat[:, :, 0:1] = jnp.full((3, 1024, 1), -1e30, F32)
    stat[:, :, 1:2] = jnp.zeros((3, 1024, 1), F32)

    def pumps(*which):
        for slot, o in which:
            pump(slot, o)

    def twins(o, *slots):
        for slot in slots:
            arrived(TWIN[slot], o)

    def w_start(n):
        w_fetched(n)
        for copy in w_own(n):
            copy.start()

    def w_pumps(n):
        w_pump(0, n)
        w_pump(1, n)

    def give(n, carry):
        psend[n] = product(0, n).astype(BF16)
        for copy in part_sends(n):
            copy.start()
        return carry

    def give_chunk(n):
        w_pump(2, n)
        w_twins(n)
        lax.fori_loop(0, 2, lambda i, carry: give(n + CHUNKS * i, carry), 0)

    fresh_arrived(0)
    fresh_arrived(2)
    pumps((UP1, 0), (DN1, 0), (XN, 0))
    fresh_start(1)
    fresh_start(3)
    w_start(0)
    twins(0, UP1, DN1)
    attend(own_a, chunk(FIRST, 0))
    pumps((UP1, 1), (DN1, 1), (XN, 1))
    w_start(1)
    attend(far_a, chunk(FIRST, 0))
    w_start(2)
    twins(1, UP1, DN1)
    attend(own_1, chunk(FIRST, 1))
    pumps((UP2, 0), (XUP1, 0))
    w_start(3)

    arrived(SIB, 0)
    twins(0, XN, UP2)
    attend(own_a, chunk(SECOND, 0))
    pumps((XDN1, 0), (UP2, 1), (XUP1, 1))
    attend(far_a, chunk(SECOND, 0))
    pumps((XDN1, 1))
    w_pumps(0)
    arrived(SIB, 1)
    twins(1, XN, UP2)
    attend(own_1, chunk(SECOND, 1))

    twins(0, XUP1, XDN1)
    attend(far_a, chunk(THIRD, 0))
    w_pumps(1)
    attend(own_a, chunk(THIRD, 0))
    twins(1, XUP1, XDN1)
    attend(own_1, chunk(THIRD, 1))

    pumps((XUP2, 0))
    fresh_arrived(3)
    far_cache.start()
    own_stale.wait()
    attend_piece(far_a, extra)
    pumps((XUP2, 1))
    w_pumps(2)
    fresh_arrived(1)
    next_cache.start()
    attend_piece(own_1, pair(OWN, 1 - xl))
    attend_piece(own_a, pair(OWN, xl))

    twins(0, XUP2)
    attend_piece(far_a, pair(XUP2, xl))
    finish(2)
    twins(1, XUP2)
    attend_piece(own_1, pair(XUP2, 1 - xl))
    finish(1)
    w_pumps(3)
    attend_piece(own_a, pair(XUP2, xl))
    finish(0)
    att_arrived(0)
    give_chunk(0)
    for n in range(1, CHUNKS):
        give_chunk(n)
    residual.wait()
    att_arrived(1)

    def take(n, carry):
        mine = product(1, n)
        for copy in part_sends(n):
            copy.wait_recv()
        cols = pl.ds(pl.multiple_of(n * TILE, TILE), TILE)
        summed = mine + prec[n].astype(F32)
        res[:, cols] = (res[:, cols].astype(F32) + gate[:, cols] * summed).astype(BF16)
        return carry
    lax.fori_loop(0, TILES, take, 0)

    result = pltpu.make_async_copy(res, out, loc.at[11])
    result.start()

    result.wait()
    next_cache.wait()
    far_cache.wait()
    for kind in range(4):
        for k in range(8):
            if k > 0 or kind > 1:
                fresh_send(kind, k).wait_send()
    for o in range(2):
        for copy in own_sends(o):
            copy.wait_send()
        for slot in TWIN:
            for copy in slot_sends(slot, o):
                copy.wait_send()
    for n in range(CHUNKS):
        for copy in w_own(n):
            copy.wait_send()
        for i in range(3):
            for copy in w_sends(i, n):
                copy.wait_send()
    for unit in range(3):
        att_each(lambda copy: None, lambda copy: copy.wait_send(), unit)

    def sent(n, carry):
        for copy in part_sends(n):
            copy.wait_send()
        return carry
    lax.fori_loop(0, TILES, sent, 0)


def block(fresh, stale, weight, stream, gate):
    any_ = pl.BlockSpec(memory_space=pl.ANY)
    vmem = pl.BlockSpec(memory_space=pltpu.VMEM)
    dma = pltpu.SemaphoreType.DMA
    return pl.pallas_call(
        block_kernel,
        out_shape=[jax.ShapeDtypeStruct((128, 5120), BF16),
                   jax.ShapeDtypeStruct((3, 2, 1024, 128), BF16)],
        in_specs=[any_, any_, any_, any_, vmem],
        out_specs=[any_, any_],
        scratch_shapes=[
            pltpu.VMEM((16, 2, 2, 1024, 128), BF16),
            pltpu.VMEM((2, 2, 1024, 128), BF16),
            pltpu.VMEM((3, 1024, 128), BF16),
            pltpu.VMEM((3, 1024, 128), F32),
            pltpu.VMEM((3, 1024, 2), F32),
            pltpu.VMEM((1536, 5120), BF16),
            pltpu.VMEM((2, 4, 3, 128, 128), BF16),
            pltpu.VMEM((128, 5120), BF16),
            pltpu.VMEM((TILES, 128, TILE), BF16),
            pltpu.VMEM((TILES, 128, TILE), BF16),
            dma((N_SENDS, 2)), dma((16, 2)),
            dma((4, 8)), dma((4, 8)),
            dma((7, CHUNKS)), dma((7, CHUNKS)),
            dma((4, CHUNKS)), dma((2, CHUNKS)),
            dma((3, 8, 2)), dma((2, 4, 3, 2)),
            dma((2, TILES)), dma((2, TILES)),
            dma((12,)),
        ],
        compiler_params=pltpu.CompilerParams(
            collective_id=0, has_side_effects=True, vmem_limit_bytes=62 * 2**20),
        name="gather_attend",
    )(fresh, stale, weight, stream, gate)


def per_device(fresh_qkv, stale_cache, out_weight, stream, gate_scale):
    fresh = jnp.transpose(fresh_qkv.reshape(128, 3, 8, 3, 128), (2, 3, 1, 0, 4))
    stale = jnp.transpose(stale_cache, (2, 1, 0, 3))
    block_out, cache = block(fresh, stale, out_weight, stream, gate_scale.reshape(1, -1))
    return (block_out, jnp.transpose(cache, (2, 1, 0, 3)))


def solution(mesh):
    return jax.shard_map(
        per_device,
        mesh=mesh,
        in_specs=(
            P(("patch", "head"), None, None, None),
            P("patch", None, "head", None),
            P("head", None),
            P(("patch", "head"), None),
            P(),
        ),
        out_specs=(P(("patch", "head"), None), P("patch", None, "head", None)),
        check_vma=False,
    )
```
